32 devices in a mesh: grp: 4 (over y, x), fac: 8 (over z, core).
Axes of the slice: x: 2, y: 2, z: 4, core: 2. Of those that a mesh axis runs over, the one named last changes fastest.
Arguments:
- image_cube: float32 [32, 1536, 256], P('fac', 'grp'), may hold values from -6 to 6
- dual: bfloat16 [8, 32, 2304, 256], P(None, None, ('grp', 'fac')), may hold values from -6 to 6
- lowpass: bfloat16 [2, 4], replicated, may hold values from -2.5 to 2.5, as said below
- thresholds: float32 [8], replicated, may hold values from 4 to 16
- facet_rows: int32 [4, 8], replicated, may hold values from 24 to 72, as said below
Outputs:
- dual_next: bfloat16 [8, 32, 2304, 256], P(None, None, ('grp', 'fac'))
- prior_term: float32 [32, 1536, 256], P('fac', 'grp')
The draws below stay inside these ranges and needn't reach their ends.
Inputs may be any that keep to these rules, and one draw needn't show every extreme that they name: `facet_rows`: every row sums to 384; in every row some facet has exactly 72 rows and some exactly 24. `lowpass`: row d has nonzero taps only at positions 2 - d - 1 to 2 + d.
All inputs are finite; a program needn't handle non-finite values.
Results may differ from the reference program's by a relative error of at most 0.0035.
Values sent between devices are 32-bit elements; how exact they have to be, the bound alone decides.
A program may use at most 128 MiB of HBM per device.

```python
import math
import jax
import jax.numpy as jnp
from jax import lax

C = 32
NDICT = 2
RMEAN = 48
W = 256
RCAP = 72
BANDS = 4
FACETS = 8
NROWS = 1536
SLOTS = 2304
NSUB = 8


def draw_lowpass(key, part):
    tap_positions = jnp.arange(2 * NDICT)
    half_widths = jnp.arange(NDICT) + 1
    support = (tap_positions[None, :] >= NDICT - half_widths[:, None]) & (tap_positions[None, :] < NDICT + half_widths[:, None])
    samples = jnp.clip(jax.random.normal(key, (NDICT, 2 * NDICT), jnp.float32), -3.5, 3.5)
    scaled = jnp.where(support, samples, 0.0) / jnp.sqrt(2.0 * half_widths.astype(jnp.float32))[:, None]
    return scaled.astype(jnp.bfloat16)


def draw_facet_rows(key, part):
    first_key = jax.random.fold_in(key, 11)
    second_key = jax.random.fold_in(key, 23)
    spread_rows = RMEAN // 2
    pairs = FACETS // 2
    shifts_drawn = jax.random.randint(first_key, (BANDS, pairs), -spread_rows, spread_rows + 1)
    forced_pair = jax.random.randint(second_key, (BANDS, 1), 0, pairs)
    shifts_drawn = jnp.where(jnp.arange(pairs)[None, :] == forced_pair, spread_rows, shifts_drawn)
    lengths = jnp.stack([RMEAN + shifts_drawn, RMEAN - shifts_drawn], axis=-1).reshape(BANDS, FACETS)
    return lengths.astype(jnp.int32)


def level_of(rng, dims, cuts, low, largest):
    def one(dim, blocks):
        steps = jax.random.uniform(jax.random.fold_in(jax.random.fold_in(rng, 6), dim), (blocks,), jnp.float32, low / len(cuts), largest / len(cuts))
        return jnp.repeat(jnp.exp(steps), dims[dim] // blocks).reshape((-1,) + (1,) * (len(dims) - dim - 1))

    level = one(*cuts[0])
    for cut in cuts[1:]:
        level = level * one(*cut)
    return level


def gaussian(rng, dims, width, bound, shards=(), kind=jnp.bfloat16):
    gain = level_of(rng, dims, shards, -0.22, 0.18) if shards else 1.0
    result = jax.random.normal(rng, dims, jnp.float32) * width * gain
    return jnp.minimum(jnp.maximum(result, -bound), bound).astype(kind)


def setup_inputs(seed: int = 0) -> dict:
    arg_keys = jax.random.split(jax.random.key(seed), 6)
    return {
        "image_cube": gaussian(arg_keys[0], (C, NROWS, W), 1.0, 6.0, ((0, 8), (1, 4)), jnp.float32),
        "dual": gaussian(arg_keys[1], (NSUB, C, SLOTS, W), 1.0, 6.0, ((2, 32),)),
        "lowpass": draw_lowpass(jax.random.fold_in(arg_keys[5], 71), 0),
        "thresholds": jnp.clip(jnp.exp(jax.random.uniform(arg_keys[3], (NSUB,), jnp.float32, math.log(4.0), math.log(16.0))), 4.0, 16.0),
        "facet_rows": draw_facet_rows(jax.random.fold_in(arg_keys[5], 71), 0),
    }


def highpass(lowpass_row):
    tap_count = lowpass_row.shape[0]
    parity = jnp.where(jnp.arange(tap_count) % 2 == 0, 1.0, -1.0).astype(jnp.float32)
    return parity * lowpass_row[::-1]

def forward_conv(source, filter_taps, along):
    halo_rows = filter_taps.shape[0] // 2
    length = source.shape[along]
    widths = [(0, 0)] * source.ndim
    widths[along] = (halo_rows, halo_rows)
    padded = jnp.pad(source, widths)
    summed = jnp.zeros_like(source)
    for offset in range(2 * halo_rows):
        summed = summed + filter_taps[offset] * lax.slice_in_dim(padded, offset, offset + length, axis=along)
    return summed

def adjoint_conv(source, filter_taps, along):
    halo_rows = filter_taps.shape[0] // 2
    length = source.shape[along]
    widths = [(0, 0)] * source.ndim
    widths[along] = (halo_rows, halo_rows)
    padded = jnp.pad(source, widths)
    summed = jnp.zeros_like(source)
    for offset in range(2 * halo_rows):
        begin = 2 * halo_rows - offset
        summed = summed + filter_taps[offset] * lax.slice_in_dim(padded, begin, begin + length, axis=along)
    return summed

def reference(image_cube, dual, lowpass, thresholds, facet_rows):
    filters_wide = lowpass.astype(jnp.float32)
    lengths = facet_rows.reshape(-1).astype(jnp.int32)
    starts = jnp.cumsum(lengths) - lengths
    positions = jnp.arange(RCAP, dtype=jnp.int32)
    slot_rows = (starts[:, None] + positions[None, :]).reshape(-1)
    slot_rows = jnp.clip(slot_rows, 0, NROWS - 1).astype(jnp.int32)
    slot_valid = (positions[None, :] < lengths[:, None]).reshape(-1)
    slot_mask = slot_valid.astype(jnp.float32)[None, :, None]
    row_numbers = jnp.arange(NROWS, dtype=jnp.int32)
    owner_facet = lax.optimization_barrier(jnp.sum((starts[None, :] <= row_numbers[:, None]).astype(jnp.int32), axis=1)) - 1
    row_slots = (owner_facet * RCAP + row_numbers - starts[owner_facet]).astype(jnp.int32)
    prior_term = jnp.zeros((C, NROWS, W), jnp.float32)
    updated = []
    for dict_index in range(NDICT):
        low_taps = filters_wide[dict_index]
        filter_pair = [low_taps, highpass(low_taps)]
        filtered = [forward_conv(image_cube, filter_pair[kind], 2) for kind in range(2)]
        row_sums = [jnp.zeros((C, NROWS, W), jnp.float32), jnp.zeros((C, NROWS, W), jnp.float32)]
        for row_kind in range(2):
            for column_kind in range(2):
                subband = 4 * dict_index + 2 * row_kind + column_kind
                coefficient = forward_conv(filtered[column_kind], filter_pair[row_kind], 1)
                combined = (dual[subband].astype(jnp.float32) + coefficient[:, slot_rows, :]) * slot_mask
                magnitude = jnp.sqrt(lax.optimization_barrier(jnp.sum(combined * combined, axis=0)))
                radius = thresholds[subband]
                scaled = (combined * (radius / jnp.maximum(magnitude, radius))).astype(jnp.bfloat16)
                updated.append(scaled)
                restored = scaled[:, row_slots, :].astype(jnp.float32)
                row_sums[column_kind] = row_sums[column_kind] + adjoint_conv(restored, filter_pair[row_kind], 1)
        for column_kind in range(2):
            prior_term = prior_term + adjoint_conv(row_sums[column_kind], filter_pair[column_kind], 2)
    return (jnp.stack(updated, 0), prior_term)
```

```python
import functools

import jax
import jax.numpy as jnp
from jax import lax
from jax.experimental import pallas as pl
from jax.experimental.pallas import tpu as pltpu
from jax.sharding import PartitionSpec as P

HALO = 2
LEAD = 8
F32 = jnp.float32
BF16 = jnp.bfloat16


def shifted(x, axis, by):
    devices = lax.axis_size(axis)
    pairs = [(i, i + by) for i in range(devices) if 0 <= i + by < devices]
    return lax.ppermute(x, axis, pairs)


def cut_kernel(cap, starts_ref, image_ref, above_ref, below_ref, out_ref, padded):
    rows = image_ref.shape[1]
    padded[:, 0:LEAD, :] = jnp.zeros_like(padded[:, 0:LEAD, :])
    tail = padded.shape[1] - LEAD - rows
    padded[:, LEAD + rows :, :] = jnp.zeros((padded.shape[0], tail, padded.shape[2]), F32)
    padded[:, LEAD : LEAD + rows, :] = image_ref[...]
    padded[:, LEAD - HALO : LEAD, :] = above_ref[...]
    padded[:, LEAD + rows : LEAD + rows + HALO, :] = below_ref[...]

    @pl.loop(0, out_ref.shape[0])
    def _(pair):
        begin = starts_ref[pair] + (LEAD - HALO)
        base = pl.multiple_of((begin // 8) * 8, 8)
        turn = cap + 8 - (begin - base)

        @pl.loop(0, out_ref.shape[1])
        def _(channel):
            window = padded[channel, pl.ds(base, cap + 8), :]
            out_ref[pair, channel] = pltpu.roll(window, turn, 0)[:cap]


def cut(starts, image, above, below, pairs, cap):
    channels, rows, columns = image.shape
    vmem = pl.BlockSpec(memory_space=pltpu.VMEM)
    return pl.pallas_call(
        functools.partial(cut_kernel, cap),
        out_shape=jax.ShapeDtypeStruct((pairs, channels, cap, columns), F32),
        in_specs=[pl.BlockSpec(memory_space=pltpu.SMEM), vmem, vmem, vmem],
        out_specs=vmem,
        scratch_shapes=[pltpu.VMEM((channels, LEAD + rows + cap + 16, columns), F32)],
        compiler_params=pltpu.CompilerParams(vmem_limit_bytes=48 * 2**20),
    )(starts, image, above, below)


def join_kernel(cap, starts_ref, windows_ref, above_ref, below_ref, out_ref, padded):
    rows = out_ref.shape[1]
    padded[...] = jnp.zeros_like(padded)

    @pl.loop(0, windows_ref.shape[0])
    def _(pair):
        begin = starts_ref[pair] + (LEAD - HALO)
        base = pl.multiple_of((begin // 8) * 8, 8)

        @pl.loop(0, windows_ref.shape[1])
        def _(channel):
            window = windows_ref[pair, channel]
            window = jnp.concatenate([window, jnp.zeros((8, window.shape[1]), F32)], 0)
            here = (channel, pl.ds(base, cap + 8), slice(None))
            padded[here] = padded[here] + pltpu.roll(window, begin - base, 0)

    out_ref[...] = padded[:, LEAD : LEAD + rows, :]
    out_ref[:, 0:HALO, :] = out_ref[:, 0:HALO, :] + above_ref[...]
    out_ref[:, rows - HALO : rows, :] = out_ref[:, rows - HALO : rows, :] + below_ref[...]


def join(starts, windows, above, below, rows):
    pairs, channels, cap, columns = windows.shape
    vmem = pl.BlockSpec(memory_space=pltpu.VMEM)
    return pl.pallas_call(
        functools.partial(join_kernel, cap),
        out_shape=jax.ShapeDtypeStruct((channels, rows, columns), F32),
        in_specs=[pl.BlockSpec(memory_space=pltpu.SMEM), vmem, vmem, vmem],
        out_specs=vmem,
        scratch_shapes=[pltpu.VMEM((channels, LEAD + rows + cap + 16, columns), F32)],
        compiler_params=pltpu.CompilerParams(vmem_limit_bytes=48 * 2**20),
    )(starts, windows, above, below)


GROUP = 8


def prox_kernel(
    facts_ref, taps_ref, thresholds_ref, own_ref, other_ref, ahead_ref, back_ref, dual_ref,
    next_ref, own_out, other_out, image, terms, wide,
):
    step = pl.program_id(0)
    kinds = pl.num_programs(0)
    core, offset, length = facts_ref[0], facts_ref[1], facts_ref[2]
    channels, capacity, columns = dual_ref.shape[1:]
    chips, share, cap, _ = own_ref.shape
    span = capacity + 16
    base = pl.multiple_of(jnp.minimum((offset // 8) * 8, cap - span), 8)
    shift = offset - base
    flat = GROUP * capacity

    @pl.when(step == 0)
    def _():
        for source, half in ((own_ref, core), (other_ref, 1 - core)):
            @pl.loop(0, chips * share)
            def _(i):
                chip, channel = i // share, i % share
                window = source[chip, channel, pl.ds(base, span), :]
                turned = pltpu.roll(window, span - shift, 0)
                image[(2 * chip + half) * share + channel] = turned[: capacity + 8]

    keep = lax.broadcasted_iota(jnp.int32, (capacity, columns), 0) < length

    def analysis(group, sums):
        begin = pl.multiple_of(group * GROUP, GROUP)
        rows = taps_ref[step, 0] * image[pl.ds(begin, GROUP), 0:capacity, :]
        for k in range(1, 2 * HALO):
            rows += taps_ref[step, k] * image[pl.ds(begin, GROUP), k : k + capacity, :]
        rows = rows.reshape(flat, columns)
        high = rows.astype(BF16)
        low = (rows - high.astype(F32)).astype(BF16)
        both = jnp.concatenate([high, low], axis=1)
        coefficient = jnp.dot(both, ahead_ref[0], preferred_element_type=F32)
        out = []
        for b in range(2):
            part = coefficient[:, b * columns : (b + 1) * columns]
            part = part.reshape(GROUP, capacity, columns)
            u = dual_ref[b, pl.ds(begin, GROUP)].astype(F32) + part
            u = jnp.where(keep, u, 0.0)
            wide[b, pl.ds(begin, GROUP)] = u
            out.append(sums[b] + jnp.sum(u * u, axis=0))
        return tuple(out)

    zero = jnp.zeros((capacity, columns), F32)
    sums = lax.fori_loop(0, channels // GROUP, analysis, (zero, zero))
    scales = []
    for b in range(2):
        radius = thresholds_ref[2 * step + b]
        scales.append(radius / jnp.maximum(jnp.sqrt(sums[b]), radius))

    @pl.loop(0, channels // GROUP)
    def _(group):
        begin = pl.multiple_of(group * GROUP, GROUP)
        parts = []
        for b in range(2):
            scaled = (wide[b, pl.ds(begin, GROUP)] * scales[b]).astype(BF16)
            next_ref[b, pl.ds(begin, GROUP)] = scaled
            parts.append(scaled.reshape(flat, columns))
        both = jnp.concatenate(parts, axis=1)
        term = jnp.dot(both, back_ref[0], preferred_element_type=F32)
        terms[step, pl.ds(begin, GROUP)] = term.reshape(GROUP, capacity, columns)

    @pl.when(step == kinds - 1)
    def _():
        for target, half in ((own_out, core), (other_out, 1 - core)):
            target[...] = jnp.zeros_like(target)

            @pl.loop(0, chips * share)
            def _(i):
                chip, channel = i // share, i % share
                at = (2 * chip + half) * share + channel
                loaded = [terms[j, at] for j in range(terms.shape[0])]
                merged = jnp.zeros((span, columns), F32)
                for k in range(2 * HALO):
                    tap_sum = taps_ref[0, k] * loaded[0]
                    for j in range(1, len(loaded)):
                        tap_sum += taps_ref[j, k] * loaded[j]
                    tail = jnp.zeros((span - capacity, columns), F32)
                    tall = jnp.concatenate([tap_sum, tail], 0)
                    merged += pltpu.roll(tall, k, 0) if k else tall
                target[chip, channel, pl.ds(base, span), :] = pltpu.roll(merged, shift, 0)


def prox(facts, taps, thresholds, own, other, ahead, back, dual):
    subbands, channels, capacity, columns = dual.shape
    kinds = subbands // 2
    smem = pl.BlockSpec(memory_space=pltpu.SMEM)
    vmem = pl.BlockSpec(memory_space=pltpu.VMEM)
    per_dict = pl.BlockSpec((1, 2 * columns, 2 * columns), lambda i: (i // 2, 0, 0))
    per_dict_back = pl.BlockSpec((1, 2 * columns, columns), lambda i: (i // 2, 0, 0))
    block = pl.BlockSpec((2, channels, capacity, columns), lambda i: (i, 0, 0, 0))
    return pl.pallas_call(
        prox_kernel,
        grid=(kinds,),
        out_shape=(
            jax.ShapeDtypeStruct(dual.shape, dual.dtype),
            jax.ShapeDtypeStruct(own.shape, F32),
            jax.ShapeDtypeStruct(own.shape, F32),
        ),
        in_specs=[smem, smem, smem, vmem, vmem, per_dict, per_dict_back, block],
        out_specs=(block, vmem, vmem),
        scratch_shapes=[
            pltpu.VMEM((channels, capacity + 8, columns), F32),
            pltpu.VMEM((kinds, channels, capacity, columns), F32),
            pltpu.VMEM((2, channels, capacity, columns), F32),
        ],
        compiler_params=pltpu.CompilerParams(vmem_limit_bytes=60 * 2**20),
    )(facts, taps, thresholds, own, other, ahead, back, dual)


def highpass(lowpass_row):
    tap_count = lowpass_row.shape[0]
    parity = jnp.where(jnp.arange(tap_count) % 2 == 0, 1.0, -1.0).astype(F32)
    return parity * lowpass_row[::-1]


def on_device(image_cube, dual, lowpass, thresholds, facet_rows):
    groups = lax.axis_size("fac")
    band_index = lax.axis_index("grp")
    facet_index = lax.axis_index("fac")
    _, band_rows, columns = image_cube.shape
    capacity = dual.shape[2]
    dicts, tap_count = lowpass.shape
    lows = lowpass.astype(F32)
    taps = jnp.stack([jnp.stack([lows[d], highpass(lows[d])]) for d in range(dicts)])
    place = jnp.arange(columns)
    offset = place[:, None] - place[None, :] + HALO
    matrix = jnp.zeros((dicts, 2, columns, columns), F32)
    for k in range(tap_count):
        matrix = matrix + jnp.where(offset == k, taps[:, :, k, None, None], 0.0)
    ahead = jnp.concatenate([matrix[:, 0], matrix[:, 1]], axis=2)
    ahead = jnp.concatenate([ahead, ahead], axis=1).astype(BF16)
    back = jnp.swapaxes(matrix, 2, 3).reshape(dicts, 2 * columns, columns).astype(BF16)
    row_taps = taps.reshape(2 * dicts, tap_count)

    lengths = lax.dynamic_index_in_dim(facet_rows, band_index, 0, keepdims=False)
    starts = jnp.cumsum(lengths) - lengths
    pairs = groups // 2
    pair_starts = starts[::2]
    core = facet_index % 2
    facet_offset = starts[facet_index] - starts[facet_index - core]
    facts = jnp.stack([core, facet_offset, lengths[facet_index]]).astype(jnp.int32)
    last_offset = band_rows - pair_starts[-1]

    above = shifted(image_cube[:, band_rows - HALO :], "grp", 1)
    below = shifted(image_cube[:, :HALO], "grp", -1)
    same_core = [list(range(c, groups, 2)) for c in range(2)]
    siblings = [(i, i ^ 1) for i in range(groups)]

    def run(cap):
        def body():
            sent = cut(pair_starts, image_cube, above, below, pairs, cap)
            own = lax.all_to_all(
                sent, "fac", split_axis=0, concat_axis=0, tiled=True, axis_index_groups=same_core
            )
            other = lax.ppermute(own, "fac", siblings)
            updated, own_out, other_out = prox(
                facts, row_taps, thresholds, own, other, ahead, back, dual
            )
            summed = own_out + lax.ppermute(other_out, "fac", siblings)
            windows = lax.all_to_all(
                summed, "fac", split_axis=0, concat_axis=0, tiled=True, axis_index_groups=same_core
            )
            spill_up = windows[0, :, :HALO]
            spill_down = lax.dynamic_slice_in_dim(windows[-1], HALO + last_offset, HALO, 1)
            from_next = shifted(spill_up, "grp", -1)
            from_previous = shifted(spill_down, "grp", 1)
            return updated, join(pair_starts, windows, from_previous, from_next, band_rows)

        return body

    most = jnp.max(facet_rows.reshape(-1, 2).sum(axis=1))
    mean = 2 * band_rows // groups
    steps = [mean, (mean + 2 * capacity) // 2, 2 * capacity]
    caps = [-(-(rows + 2 * HALO) // 8) * 8 for rows in steps]
    choice = (most > steps[0]).astype(jnp.int32) + (most > steps[1]).astype(jnp.int32)
    return lax.switch(choice, [run(cap) for cap in caps])


def solution(mesh):
    placed = (P("fac", "grp", None), P(None, None, ("grp", "fac"), None), P(), P(), P())
    return jax.shard_map(
        on_device,
        mesh=mesh,
        in_specs=placed,
        out_specs=(P(None, None, ("grp", "fac"), None), P("fac", "grp", None)),
        check_vma=False,
    )
```

```python
import functools

import jax
import jax.numpy as jnp
from jax import lax
from jax.experimental import pallas as pl
from jax.experimental.pallas import tpu as pltpu
from jax.sharding import PartitionSpec as P

HALO = 2
LEAD = 8
F32 = jnp.float32
BF16 = jnp.bfloat16
MESH = pl.DeviceIdType.MESH


def shifted(x, axis, by):
    devices = lax.axis_size(axis)
    pairs = [(i, i + by) for i in range(devices) if 0 <= i + by < devices]
    return lax.ppermute(x, axis, pairs)


def facet_starts(rows_ref):
    band = lax.axis_index("grp")
    starts = [jnp.int32(0)]
    for facet in range(rows_ref.shape[1]):
        starts.append(starts[-1] + rows_ref[band, facet])
    return starts


def cut_kernel(cap, rows_ref, image_ref, above_ref, below_ref, out_ref, padded):
    rows = image_ref.shape[1]
    padded[:, 0:LEAD, :] = jnp.zeros_like(padded[:, 0:LEAD, :])
    tail = padded.shape[1] - LEAD - rows
    padded[:, LEAD + rows :, :] = jnp.zeros((padded.shape[0], tail, padded.shape[2]), F32)
    padded[:, LEAD : LEAD + rows, :] = image_ref[...]
    padded[:, LEAD - HALO : LEAD, :] = above_ref[...]
    padded[:, LEAD + rows : LEAD + rows + HALO, :] = below_ref[...]
    starts = facet_starts(rows_ref)

    for pair in range(out_ref.shape[0]):
        begin = starts[2 * pair] + (LEAD - HALO)
        base = pl.multiple_of((begin // 8) * 8, 8)
        turn = cap + 8 - (begin - base)

        @pl.loop(0, out_ref.shape[1])
        def _(channel):
            window = padded[channel, pl.ds(base, cap + 8), :]
            out_ref[pair, channel] = pltpu.roll(window, turn, 0)[:cap]


def cut(facet_rows, image, above, below, pairs, cap):
    channels, rows, columns = image.shape
    vmem = pl.BlockSpec(memory_space=pltpu.VMEM)
    return pl.pallas_call(
        functools.partial(cut_kernel, cap),
        out_shape=jax.ShapeDtypeStruct((pairs, channels, cap, columns), F32),
        in_specs=[pl.BlockSpec(memory_space=pltpu.SMEM), vmem, vmem, vmem],
        out_specs=vmem,
        scratch_shapes=[pltpu.VMEM((channels, LEAD + rows + cap + 16, columns), F32)],
        compiler_params=pltpu.CompilerParams(vmem_limit_bytes=48 * 2**20),
    )(facet_rows, image, above, below)


def join_kernel(cap, rows_ref, windows_ref, above_ref, below_ref, out_ref, padded):
    rows = out_ref.shape[1]
    padded[...] = jnp.zeros_like(padded)
    starts = facet_starts(rows_ref)

    for pair in range(windows_ref.shape[0]):
        begin = starts[2 * pair] + (LEAD - HALO)
        base = pl.multiple_of((begin // 8) * 8, 8)

        @pl.loop(0, windows_ref.shape[1])
        def _(channel):
            window = windows_ref[pair, channel]
            window = jnp.concatenate([window, jnp.zeros((8, window.shape[1]), F32)], 0)
            here = (channel, pl.ds(base, cap + 8), slice(None))
            padded[here] = padded[here] + pltpu.roll(window, begin - base, 0)

    out_ref[...] = padded[:, LEAD : LEAD + rows, :]
    out_ref[:, 0:HALO, :] = out_ref[:, 0:HALO, :] + above_ref[...]
    out_ref[:, rows - HALO : rows, :] = out_ref[:, rows - HALO : rows, :] + below_ref[...]


def join(facet_rows, windows, above, below, rows):
    pairs, channels, cap, columns = windows.shape
    vmem = pl.BlockSpec(memory_space=pltpu.VMEM)
    return pl.pallas_call(
        functools.partial(join_kernel, cap),
        out_shape=jax.ShapeDtypeStruct((channels, rows, columns), F32),
        in_specs=[pl.BlockSpec(memory_space=pltpu.SMEM), vmem, vmem, vmem],
        out_specs=vmem,
        scratch_shapes=[pltpu.VMEM((channels, LEAD + rows + cap + 16, columns), F32)],
        compiler_params=pltpu.CompilerParams(vmem_limit_bytes=48 * 2**20),
    )(facet_rows, windows, above, below)


def position(chips):
    facet = lax.axis_index("fac")
    core = lax.rem(facet, 2)
    chip = lax.div(facet, 2)
    sibling = facet + 1 - 2 * core

    def at(r):
        return lax.rem(chip + r, chips)

    return core, chip, sibling, at


def greet(core, sibling, at, chips):
    barrier = pltpu.get_barrier_semaphore()
    for device in [2 * at(r) + core for r in range(1, chips)] + [sibling]:
        pl.semaphore_signal(barrier, inc=1, device_id={"fac": device}, device_id_type=MESH)
    pl.semaphore_wait(barrier, chips)


def remote(source, target, send, recv, device):
    return pltpu.make_async_remote_copy(
        src_ref=source, dst_ref=target, send_sem=send, recv_sem=recv,
        device_id={"fac": device}, device_id_type=MESH,
    )


def spread_kernel(sent, own, other, send, recv, pass_send, pass_recv, kept):
    chips, share = sent.shape[:2]
    core, chip, sibling, at = position(chips)
    greet(core, sibling, at, chips)
    home = pltpu.make_async_copy(sent.at[chip], own.at[chip], kept)
    home.start()
    outgoing, passed = [], []
    for c in range(share):
        for r in range(1, chips):
            outgoing.append(remote(
                sent.at[at(r), c], own.at[chip, c], send.at[r, c], recv.at[r, c],
                2 * at(r) + core,
            ))
            outgoing[-1].start()
        passed.append(remote(
            sent.at[chip, c], other.at[chip, c], pass_send.at[0, c], pass_recv.at[0, c], sibling
        ))
        passed[-1].start()
    for c in range(share):
        for r in range(1, chips):
            outgoing[c * (chips - 1) + r - 1].wait_recv()
            source = at(chips - r)
            passed.append(remote(
                own.at[source, c], other.at[source, c], pass_send.at[r, c], pass_recv.at[r, c],
                sibling,
            ))
            passed[-1].start()
    for copy in outgoing:
        copy.wait_send()
    for copy in passed:
        copy.wait()
    home.wait()


def spread(sent, collective_id):
    chips, share = sent.shape[:2]
    vmem = pl.BlockSpec(memory_space=pltpu.VMEM)
    shape = jax.ShapeDtypeStruct(sent.shape, F32)
    return pl.pallas_call(
        spread_kernel,
        out_shape=(shape, shape),
        in_specs=[vmem],
        out_specs=(vmem, vmem),
        scratch_shapes=[pltpu.SemaphoreType.DMA((chips, share))] * 4 + [pltpu.SemaphoreType.DMA],
        compiler_params=pltpu.CompilerParams(
            collective_id=collective_id, has_side_effects=True, vmem_limit_bytes=48 * 2**20
        ),
    )(sent)


def collect_kernel(own, other, out, arrived, total, send, recv, pass_send, pass_recv):
    chips, share = own.shape[:2]
    core, chip, sibling, at = position(chips)
    greet(core, sibling, at, chips)
    passed, outgoing = [], []
    order = [(c, r) for c in range(share) for r in list(range(1, chips)) + [0]]
    for c, r in order:
        passed.append(remote(
            other.at[at(r), c], arrived.at[at(r), c], pass_send.at[r, c], pass_recv.at[r, c],
            sibling,
        ))
        passed[-1].start()
    for copy, (c, r) in zip(passed, order):
        copy.wait_recv()
        summed = own[at(r), c] + arrived[at(r), c]
        if r == 0:
            out[chip, c] = summed
        else:
            total[at(r), c] = summed
            outgoing.append(remote(
                total.at[at(r), c], out.at[chip, c], send.at[r, c], recv.at[r, c],
                2 * at(r) + core,
            ))
            outgoing[-1].start()
    for copy in passed:
        copy.wait_send()
    for copy in outgoing:
        copy.wait()


def collect(own, other, collective_id):
    chips, share = own.shape[:2]
    vmem = pl.BlockSpec(memory_space=pltpu.VMEM)
    return pl.pallas_call(
        collect_kernel,
        out_shape=jax.ShapeDtypeStruct(own.shape, F32),
        in_specs=[vmem, vmem],
        out_specs=vmem,
        scratch_shapes=[pltpu.VMEM(own.shape, F32)] * 2
        + [pltpu.SemaphoreType.DMA((chips, share))] * 4,
        compiler_params=pltpu.CompilerParams(
            collective_id=collective_id, has_side_effects=True, vmem_limit_bytes=48 * 2**20
        ),
    )(own, other)


GROUP = 8


def tap(low_ref, d, a, k):
    count = low_ref.shape[1]
    high = low_ref[d, count - 1 - k] * (1.0 if k % 2 == 0 else -1.0)
    return jnp.where(a == 0, low_ref[d, k], high)


def prox_kernel(
    rows_ref, low_ref, thresholds_ref, own_ref, other_ref, dual_ref,
    next_ref, own_out, other_out, image, terms, wide, ahead, back,
):
    step = pl.program_id(0)
    kinds = pl.num_programs(0)
    d, a = step // 2, step % 2
    facet, band = lax.axis_index("fac"), lax.axis_index("grp")
    core = facet % 2
    offset = jnp.where(core == 0, 0, rows_ref[band, facet - core])
    length = rows_ref[band, facet]
    channels, capacity, columns = dual_ref.shape[1:]
    chips, share, cap, _ = own_ref.shape
    span = capacity + 16
    base = pl.multiple_of(jnp.minimum((offset // 8) * 8, cap - span), 8)
    shift = offset - base
    flat = GROUP * capacity

    @pl.when(a == 0)
    def _():
        into = lax.broadcasted_iota(jnp.int32, (columns, columns), 0)
        of = lax.broadcasted_iota(jnp.int32, (columns, columns), 1)
        for b in range(2):
            forward = jnp.zeros((columns, columns), F32)
            adjoint = jnp.zeros((columns, columns), F32)
            for k in range(2 * HALO):
                value = tap(low_ref, d, b, k)
                forward = jnp.where(into - of + HALO == k, value, forward)
                adjoint = jnp.where(of - into + HALO == k, value, adjoint)
            forward = forward.astype(BF16)
            ahead[0:columns, b * columns : (b + 1) * columns] = forward
            ahead[columns:, b * columns : (b + 1) * columns] = forward
            back[b * columns : (b + 1) * columns, :] = adjoint.astype(BF16)

    @pl.when(step == 0)
    def _():
        for source, half in ((own_ref, core), (other_ref, 1 - core)):
            @pl.loop(0, chips * share)
            def _(i):
                chip, channel = i // share, i % share
                window = source[chip, channel, pl.ds(base, span), :]
                turned = pltpu.roll(window, span - shift, 0)
                image[(2 * chip + half) * share + channel] = turned[: capacity + 8]

    keep = lax.broadcasted_iota(jnp.int32, (capacity, columns), 0) < length

    def analysis(group, sums):
        begin = pl.multiple_of(group * GROUP, GROUP)
        rows = tap(low_ref, d, a, 0) * image[pl.ds(begin, GROUP), 0:capacity, :]
        for k in range(1, 2 * HALO):
            rows += tap(low_ref, d, a, k) * image[pl.ds(begin, GROUP), k : k + capacity, :]
        rows = rows.reshape(flat, columns)
        high = rows.astype(BF16)
        low = (rows - high.astype(F32)).astype(BF16)
        both = jnp.concatenate([high, low], axis=1)
        coefficient = jnp.dot(both, ahead[...], preferred_element_type=F32)
        out = []
        for b in range(2):
            part = coefficient[:, b * columns : (b + 1) * columns]
            part = part.reshape(GROUP, capacity, columns)
            u = dual_ref[b, pl.ds(begin, GROUP)].astype(F32) + part
            u = jnp.where(keep, u, 0.0)
            wide[b, pl.ds(begin, GROUP)] = u
            out.append(sums[b] + jnp.sum(u * u, axis=0))
        return tuple(out)

    zero = jnp.zeros((capacity, columns), F32)
    sums = lax.fori_loop(0, channels // GROUP, analysis, (zero, zero))
    scales = []
    for b in range(2):
        radius = thresholds_ref[2 * step + b]
        scales.append(radius / jnp.maximum(jnp.sqrt(sums[b]), radius))

    @pl.loop(0, channels // GROUP)
    def _(group):
        begin = pl.multiple_of(group * GROUP, GROUP)
        parts = []
        for b in range(2):
            scaled = (wide[b, pl.ds(begin, GROUP)] * scales[b]).astype(BF16)
            next_ref[b, pl.ds(begin, GROUP)] = scaled
            parts.append(scaled.reshape(flat, columns))
        both = jnp.concatenate(parts, axis=1)
        term = jnp.dot(both, back[...], preferred_element_type=F32)
        terms[step, pl.ds(begin, GROUP)] = term.reshape(GROUP, capacity, columns)

    @pl.when(step == kinds - 1)
    def _():
        for target, half in ((own_out, core), (other_out, 1 - core)):
            target[...] = jnp.zeros_like(target)

            @pl.loop(0, chips * share)
            def _(i):
                chip, channel = i // share, i % share
                at = (2 * chip + half) * share + channel
                loaded = [terms[j, at] for j in range(terms.shape[0])]
                merged = jnp.zeros((span, columns), F32)
                for k in range(2 * HALO):
                    tap_sum = tap(low_ref, 0, 0, k) * loaded[0]
                    for j in range(1, len(loaded)):
                        tap_sum += tap(low_ref, j // 2, j % 2, k) * loaded[j]
                    tail = jnp.zeros((span - capacity, columns), F32)
                    tall = jnp.concatenate([tap_sum, tail], 0)
                    merged += pltpu.roll(tall, k, 0) if k else tall
                target[chip, channel, pl.ds(base, span), :] = pltpu.roll(merged, shift, 0)


def prox(facet_rows, lows, thresholds, own, other, dual):
    subbands, channels, capacity, columns = dual.shape
    kinds = subbands // 2
    smem = pl.BlockSpec(memory_space=pltpu.SMEM)
    vmem = pl.BlockSpec(memory_space=pltpu.VMEM)
    block = pl.BlockSpec((2, channels, capacity, columns), lambda i: (i, 0, 0, 0))
    return pl.pallas_call(
        prox_kernel,
        grid=(kinds,),
        out_shape=(
            jax.ShapeDtypeStruct(dual.shape, dual.dtype),
            jax.ShapeDtypeStruct(own.shape, F32),
            jax.ShapeDtypeStruct(own.shape, F32),
        ),
        in_specs=[smem, smem, smem, vmem, vmem, block],
        out_specs=(block, vmem, vmem),
        scratch_shapes=[
            pltpu.VMEM((channels, capacity + 8, columns), F32),
            pltpu.VMEM((kinds, channels, capacity, columns), F32),
            pltpu.VMEM((2, channels, capacity, columns), F32),
            pltpu.VMEM((2 * columns, 2 * columns), BF16),
            pltpu.VMEM((2 * columns, columns), BF16),
        ],
        compiler_params=pltpu.CompilerParams(vmem_limit_bytes=60 * 2**20),
    )(facet_rows, lows, thresholds, own, other, dual)


def on_device(image_cube, dual, lowpass, thresholds, facet_rows):
    groups = lax.axis_size("fac")
    band_index = lax.axis_index("grp")
    _, band_rows, columns = image_cube.shape
    capacity = dual.shape[2]
    pairs = groups // 2
    lows = lowpass.astype(F32)
    above = shifted(image_cube[:, band_rows - HALO :], "grp", 1)
    below = shifted(image_cube[:, :HALO], "grp", -1)

    def run(choice, cap):
        def body():
            sent = cut(facet_rows, image_cube, above, below, pairs, cap)
            own, other = spread(sent, 2 * choice)
            updated, own_out, other_out = prox(facet_rows, lows, thresholds, own, other, dual)
            windows = collect(own_out, other_out, 2 * choice + 1)
            spill_up = windows[0, :, :HALO]
            last_rows = facet_rows[band_index, -2] + facet_rows[band_index, -1]
            spill_down = lax.dynamic_slice_in_dim(windows[-1], HALO + last_rows, HALO, 1)
            from_next = shifted(spill_up, "grp", -1)
            from_previous = shifted(spill_down, "grp", 1)
            return updated, join(facet_rows, windows, from_previous, from_next, band_rows)

        return body

    most = jnp.max(facet_rows[:, ::2] + facet_rows[:, 1::2]) + 2 * HALO
    mean = 2 * band_rows // groups
    steps = [mean, (mean + 2 * capacity) // 2, 2 * capacity]
    caps = [-(-(rows + 2 * HALO) // 8) * 8 for rows in steps]
    choice = (most > caps[0]).astype(jnp.int32) + (most > caps[1]).astype(jnp.int32)
    return lax.switch(choice, [run(i, cap) for i, cap in enumerate(caps)])


def solution(mesh):
    placed = (P("fac", "grp", None), P(None, None, ("grp", "fac"), None), P(), P(), P())
    return jax.shard_map(
        on_device,
        mesh=mesh,
        in_specs=placed,
        out_specs=(P(None, None, ("grp", "fac"), None), P("fac", "grp", None)),
        check_vma=False,
    )
```

```python
import functools

import jax
import jax.numpy as jnp
from jax import lax
from jax.experimental import pallas as pl
from jax.experimental.pallas import tpu as pltpu
from jax.sharding import PartitionSpec as P

HALO = 2
LEAD = 8
F32 = jnp.float32
BF16 = jnp.bfloat16
MESH = pl.DeviceIdType.MESH


def facet_starts(rows_ref):
    band = lax.axis_index("grp")
    starts = [jnp.int32(0)]
    for facet in range(rows_ref.shape[1]):
        starts.append(starts[-1] + rows_ref[band, facet])
    return starts


def position(chips):
    facet = lax.axis_index("fac")
    core = lax.rem(facet, 2)
    chip = lax.div(facet, 2)
    sibling = facet + 1 - 2 * core

    def at(r):
        return lax.rem(chip + r, chips)

    return core, chip, sibling, at


def remote(source, target, send, recv, device):
    return pltpu.make_async_remote_copy(
        src_ref=source, dst_ref=target, send_sem=send, recv_sem=recv,
        device_id=device, device_id_type=MESH,
    )


GROUP = 8


def tap(low_ref, d, a, k):
    count = low_ref.shape[1]
    high = low_ref[d, count - 1 - k] * (1.0 if k % 2 == 0 else -1.0)
    return jnp.where(a == 0, low_ref[d, k], high)


def moved(x, amount, way):
    amounts = jnp.full(x.shape, amount, jnp.int32)
    for bit in range(7):
        if 2**bit >= x.shape[0]:
            break
        turned = pltpu.roll(x, 2**bit if way > 0 else x.shape[0] - 2**bit, 0)
        x = jnp.where((amounts & 2**bit) != 0, turned, x)
    return x


def whole_kernel(
    cap, rows_ref, low_ref, thresholds_ref, cut_ref, image_ref, dual_ref,
    next_ref, windows, above_out, below_out,
    sent, own, other, arrived, stored, wide, strips, sums, terms, ahead, back,
    edge_above, edge_below, edge_spill,
    dual_sem, next_sem, edge_send, edge_recv,
    send, recv, pass_send, pass_recv, home_send, home_recv, sum_send, sum_recv,
):
    chips, share = sent.shape[:2]
    subbands, devices, _, capacity, columns = dual_ref.shape
    kinds = subbands // 2
    rows = image_ref.shape[1]
    flat = GROUP * capacity
    span = capacity + 8
    core, chip, sibling, at = position(chips)
    facet, band = lax.axis_index("fac"), lax.axis_index("grp")
    bands = lax.axis_size("grp")
    band_next, band_last = lax.rem(band + 1, bands), lax.rem(band + bands - 1, bands)

    def same_core(r):
        return {"fac": 2 * at(r) + core}

    def dual_load(c):
        return pltpu.make_async_copy(dual_ref.at[:, :, c], stored.at[c], dual_sem.at[c])

    def next_store(c):
        return pltpu.make_async_copy(stored.at[c], next_ref.at[:, :, c], next_sem.at[c])

    def remote_to(source, target, sends, recvs, r, c, device):
        return remote(source, target, sends.at[r, c], recvs.at[r, c], device)

    def outgoing(r, c):
        return remote_to(sent.at[at(r), c], own.at[chip, c], send, recv, r, c, same_core(r))

    def incoming(r, c):
        source = at(chips - r)
        return remote_to(sent.at[source, c], own.at[source, c], send, recv, r, c, same_core(r))

    def passing(r, c):
        source = at(chips - r)
        return remote_to(
            own.at[source, c], other.at[source, c], pass_send, pass_recv, r, c, {"fac": sibling}
        )

    def homing(r, c):
        return remote_to(
            other.at[at(r), c], arrived.at[at(r), c], home_send, home_recv, r, c,
            {"fac": sibling},
        )

    def returning(r, c):
        return remote_to(
            own.at[at(r), c], windows.at[chip, c], sum_send, sum_recv, r, c, same_core(r)
        )

    def returned(r, c):
        source = at(chips - r)
        return remote_to(
            own.at[source, c], windows.at[source, c], sum_send, sum_recv, r, c, same_core(r)
        )

    barrier = pltpu.get_barrier_semaphore()
    for device in [same_core(r) for r in range(1, chips)] + [
        {"fac": sibling}, {"grp": band_next}, {"grp": band_last},
    ]:
        pl.semaphore_signal(barrier, inc=1, device_id=device, device_id_type=MESH)
    pl.semaphore_wait(barrier, chips + 2)

    rims = [
        remote(image_ref.at[:, rows - 8 : rows], edge_above, edge_send.at[0], edge_recv.at[0],
               {"grp": band_next}),
        remote(image_ref.at[:, 0:8], edge_below, edge_send.at[1], edge_recv.at[1],
               {"grp": band_last}),
    ]
    for rim in rims:
        rim.start()

    into = lax.broadcasted_iota(jnp.int32, (columns, columns), 0)
    of = lax.broadcasted_iota(jnp.int32, (columns, columns), 1)

    def build(d, _):
        for b in range(2):
            forward = jnp.zeros((columns, columns), F32)
            adjoint = jnp.zeros((columns, columns), F32)
            for k in range(2 * HALO):
                value = tap(low_ref, d, b, k)
                forward = jnp.where(into - of + HALO == k, value, forward)
                adjoint = jnp.where(of - into + HALO == k, value, adjoint)
            forward = forward.astype(BF16)
            ahead[d, 0:columns, b * columns : (b + 1) * columns] = forward
            ahead[d, columns : 2 * columns, b * columns : (b + 1) * columns] = forward
            back[d, b * columns : (b + 1) * columns, :] = adjoint.astype(BF16)
        return 0

    starts = facet_starts(rows_ref)
    last_rows = starts[2 * chips] - starts[2 * chips - 2]
    for rim in rims:
        rim.wait()
    row = lax.broadcasted_iota(jnp.int32, (cap, columns), 0)

    def rimmed(pair, c):
        window = cut_ref[pair, c]
        fill = jnp.zeros((cap - HALO, columns), F32)
        above = jnp.concatenate([edge_above[c, 8 - HALO : 8, :], fill], 0)
        first = (row < HALO) & (pair == 0) & (band > 0)
        window = jnp.where(first, above, window)
        for i in range(HALO - 1):
            below = jnp.broadcast_to(edge_below[c, i : i + 1, :], (cap, columns))
            last = (row == HALO + last_rows + i) & (pair == chips - 1) & (band < bands - 1)
            window = jnp.where(last, below, window)
        return window

    def cut(c, _):
        for r in list(range(1, chips)) + [0]:
            if r:
                sent[at(r), c] = rimmed(at(r), c)
                outgoing(r, c).start()
            else:
                own[chip, c] = rimmed(chip, c)
                passing(0, c).start()
        return 0

    lax.fori_loop(0, share, cut, 0)
    for c in range(share):
        dual_load(c).start()
    lax.fori_loop(0, low_ref.shape[0], build, 0)
    sums[...] = jnp.zeros_like(sums)

    offset = jnp.where(core == 0, 0, rows_ref[band, facet - core])
    length = rows_ref[band, facet]
    keep = lax.broadcasted_iota(jnp.int32, (capacity, columns), 0) < length

    def analyse(c, _):
        for r in range(1, chips):
            incoming(r, c).wait_recv()
            passing(r, c).start()
        for r in range(chips):
            passing(r, c).wait_recv()
        dual_load(c).wait()
        for g in range(devices // GROUP):
            for source, half in ((own, core), (other, 1 - core)):
                for j in range(GROUP // 2):
                    window = source[g * (GROUP // 2) + j, c]
                    strips[2 * j + half] = moved(window, offset, -1)[:span]

            def one_kind(step, _):
                d, a = step // 2, step % 2
                sent_rows = tap(low_ref, d, a, 0) * strips[:, 0:capacity, :]
                for k in range(1, 2 * HALO):
                    sent_rows += tap(low_ref, d, a, k) * strips[:, k : k + capacity, :]
                flat_rows = sent_rows.reshape(flat, columns)
                high = flat_rows.astype(BF16)
                low = (flat_rows - high.astype(F32)).astype(BF16)
                both = jnp.concatenate([high, low], axis=1)
                coefficient = jnp.dot(both, ahead[d], preferred_element_type=F32)
                for b in range(2):
                    part = coefficient[:, b * columns : (b + 1) * columns]
                    part = part.reshape(GROUP, capacity, columns)
                    here = pl.ds(g * GROUP, GROUP)
                    u = stored[c, 2 * step + b, here].astype(F32) + part
                    u = jnp.where(keep, u, 0.0)
                    wide[c, 2 * step + b, here] = u
                    sums[2 * step + b] += jnp.sum(u * u, axis=0)
                return 0

            lax.fori_loop(0, kinds, one_kind, 0)
        return 0

    lax.fori_loop(0, share, analyse, 0)

    def scale(s, _):
        radius = thresholds_ref[s]
        sums[s] = radius / jnp.maximum(jnp.sqrt(sums[s]), radius)
        return 0

    lax.fori_loop(0, subbands, scale, 0)

    def settle(c, _):
        for r in range(chips):
            passing(r, c).wait_send()
            if r:
                outgoing(r, c).wait_send()
        return 0

    lax.fori_loop(0, share, settle, 0)

    def synthesise(c, _):
        for g in range(devices // GROUP):
            here = pl.ds(g * GROUP, GROUP)

            def one_kind(step, _):
                parts = []
                for b in range(2):
                    scaled = (wide[c, 2 * step + b, here] * sums[2 * step + b]).astype(BF16)
                    stored[c, 2 * step + b, here] = scaled
                    parts.append(scaled.reshape(flat, columns))
                both = jnp.concatenate(parts, axis=1)
                term = jnp.dot(both, back[step // 2], preferred_element_type=F32)
                terms[step] = term.reshape(GROUP, capacity, columns)
                return 0

            lax.fori_loop(0, kinds, one_kind, 0)
            for target, half in ((own, core), (other, 1 - core)):
                def place(j, _, target=target, half=half):
                    loaded = [terms[step, 2 * j + half] for step in range(kinds)]
                    merged = jnp.zeros((span, columns), F32)
                    for k in range(2 * HALO):
                        tap_sum = tap(low_ref, 0, 0, k) * loaded[0]
                        for step in range(1, kinds):
                            tap_sum += tap(low_ref, step // 2, step % 2, k) * loaded[step]
                        spare = jnp.zeros((span - capacity, columns), F32)
                        tall = jnp.concatenate([tap_sum, spare], 0)
                        merged += pltpu.roll(tall, k, 0) if k else tall
                    merged = jnp.concatenate([merged, jnp.zeros((cap - span, columns), F32)], 0)
                    target[g * (GROUP // 2) + j, c] = moved(merged, offset, 1)
                    return 0

                lax.fori_loop(0, GROUP // 2, place, 0)
        for r in list(range(1, chips)) + [0]:
            homing(r, c).start()
        next_store(c).start()
        for r in list(range(1, chips)) + [0]:
            homing(r, c).wait_recv()
            if r:
                own[at(r), c] = own[at(r), c] + arrived[at(r), c]
                returning(r, c).start()
            else:
                windows[chip, c] = own[chip, c] + arrived[chip, c]
        return 0

    lax.fori_loop(0, share, synthesise, 0)

    def finish(c, _):
        for r in range(chips):
            homing(r, c).wait_send()
            if r:
                returned(r, c).wait_recv()
                returning(r, c).wait_send()
        next_store(c).wait()
        return 0

    lax.fori_loop(0, share, finish, 0)

    for c in range(share):
        edge_spill[c] = jnp.zeros((8, columns), F32)
        for i in range(HALO - 1):
            found = jnp.where(row == HALO + last_rows + i, windows[chips - 1, c], 0.0)
            edge_spill[c, i : i + 1, :] = jnp.sum(found, axis=0, keepdims=True)
    spills = [
        remote(edge_spill, above_out, edge_send.at[2], edge_recv.at[2], {"grp": band_next}),
        remote(windows.at[0, :, 0:8], below_out, edge_send.at[3], edge_recv.at[3],
               {"grp": band_last}),
    ]
    for spill in spills:
        spill.start()
    for spill in spills:
        spill.wait()


def whole(facet_rows, lows, thresholds, pieces, image, dual, cap, collective_id):
    subbands, devices, share, capacity, columns = dual.shape
    chips, kinds = devices // 2, subbands // 2
    smem = pl.BlockSpec(memory_space=pltpu.SMEM)
    vmem = pl.BlockSpec(memory_space=pltpu.VMEM)
    free = pl.BlockSpec(memory_space=pl.ANY)
    windows = (chips, share, cap, columns)
    rim = jax.ShapeDtypeStruct((share, 8, columns), F32)
    dma = pltpu.SemaphoreType.DMA
    return pl.pallas_call(
        functools.partial(whole_kernel, cap),
        out_shape=(
            jax.ShapeDtypeStruct(dual.shape, dual.dtype), jax.ShapeDtypeStruct(windows, F32),
            rim, rim,
        ),
        in_specs=[smem, smem, smem, vmem, free, free],
        out_specs=(free, vmem, vmem, vmem),
        scratch_shapes=[
            *[pltpu.VMEM(windows, F32)] * 4,
            pltpu.VMEM((share, subbands, devices, capacity, columns), BF16),
            pltpu.VMEM((share, subbands, devices, capacity, columns), F32),
            pltpu.VMEM((GROUP, capacity + 8, columns), F32),
            pltpu.VMEM((subbands, capacity, columns), F32),
            pltpu.VMEM((kinds, GROUP, capacity, columns), F32),
            pltpu.VMEM((kinds // 2, 2 * columns, 2 * columns), BF16),
            pltpu.VMEM((kinds // 2, 2 * columns, columns), BF16),
            *[pltpu.VMEM((share, 8, columns), F32)] * 3,
            dma((share,)), dma((share,)), dma((4,)), dma((4,)),
            *[dma((chips, share))] * 8,
        ],
        compiler_params=pltpu.CompilerParams(
            collective_id=collective_id, has_side_effects=True, vmem_limit_bytes=62 * 2**20
        ),
    )(facet_rows, lows, thresholds, pieces, image, dual)


def cut_kernel(cap, rows_ref, image_ref, out_ref, padded):
    rows = image_ref.shape[1]
    share, _, columns = padded.shape
    padded[:, 0:LEAD, :] = jnp.zeros((share, LEAD, columns), F32)
    tail = padded.shape[1] - LEAD - rows
    padded[:, LEAD + rows :, :] = jnp.zeros((share, tail, columns), F32)
    padded[:, LEAD : LEAD + rows, :] = image_ref[...]
    starts = facet_starts(rows_ref)

    for pair in range(out_ref.shape[0]):
        begin = starts[2 * pair] + (LEAD - HALO)
        base = pl.multiple_of((begin // 8) * 8, 8)
        turn = cap + 8 - (begin - base)

        @pl.loop(0, out_ref.shape[1])
        def _(channel):
            window = padded[channel, pl.ds(base, cap + 8), :]
            out_ref[pair, channel] = pltpu.roll(window, turn, 0)[:cap]


def cut(facet_rows, image, pairs, cap):
    channels, rows, columns = image.shape
    vmem = pl.BlockSpec(memory_space=pltpu.VMEM)
    return pl.pallas_call(
        functools.partial(cut_kernel, cap),
        out_shape=jax.ShapeDtypeStruct((pairs, channels, cap, columns), F32),
        in_specs=[pl.BlockSpec(memory_space=pltpu.SMEM), vmem],
        out_specs=vmem,
        scratch_shapes=[pltpu.VMEM((channels, LEAD + rows + cap + 16, columns), F32)],
        compiler_params=pltpu.CompilerParams(vmem_limit_bytes=48 * 2**20),
    )(facet_rows, image)


def join_kernel(
    cap, rows_ref, windows_ref, above_ref, below_ref, made_ref, out_ref, next_ref, padded, sems
):
    rows = out_ref.shape[1]
    moves = [
        pltpu.make_async_copy(made_ref.at[s], next_ref.at[s], sems.at[s])
        for s in range(made_ref.shape[0])
    ]
    for move in moves:
        move.start()
    padded[...] = jnp.zeros_like(padded)
    starts = facet_starts(rows_ref)
    band, bands = lax.axis_index("grp"), lax.axis_size("grp")

    for pair in range(windows_ref.shape[0]):
        begin = starts[2 * pair] + (LEAD - HALO)
        base = pl.multiple_of((begin // 8) * 8, 8)

        @pl.loop(0, windows_ref.shape[1])
        def _(channel):
            window = windows_ref[pair, channel]
            window = jnp.concatenate([window, jnp.zeros((8, window.shape[1]), F32)], 0)
            here = (channel, pl.ds(base, cap + 8), slice(None))
            padded[here] = padded[here] + pltpu.roll(window, begin - base, 0)

    out_ref[...] = padded[:, LEAD : LEAD + rows, :]
    above = jnp.where(band > 0, above_ref[:, 0:HALO, :], 0.0)
    below = jnp.where(band < bands - 1, below_ref[:, 0:HALO, :], 0.0)
    out_ref[:, 0:HALO, :] = out_ref[:, 0:HALO, :] + above
    out_ref[:, rows - HALO : rows, :] = out_ref[:, rows - HALO : rows, :] + below
    for move in moves:
        move.wait()


def join(facet_rows, windows, above, below, made, rows):
    pairs, channels, cap, columns = windows.shape
    vmem = pl.BlockSpec(memory_space=pltpu.VMEM)
    free = pl.BlockSpec(memory_space=pl.ANY)
    return pl.pallas_call(
        functools.partial(join_kernel, cap),
        out_shape=(
            jax.ShapeDtypeStruct((channels, rows, columns), F32),
            jax.ShapeDtypeStruct(made.shape, made.dtype),
        ),
        in_specs=[pl.BlockSpec(memory_space=pltpu.SMEM), vmem, vmem, vmem, free],
        out_specs=(vmem, free),
        scratch_shapes=[
            pltpu.VMEM((channels, LEAD + rows + cap + 16, columns), F32),
            pltpu.SemaphoreType.DMA((made.shape[0],)),
        ],
        compiler_params=pltpu.CompilerParams(vmem_limit_bytes=48 * 2**20),
    )(facet_rows, windows, above, below, made)


def on_device(image_cube, dual, lowpass, thresholds, facet_rows):
    groups = lax.axis_size("fac")
    share, band_rows, _ = image_cube.shape
    subbands, _, capacity, columns = dual.shape
    lows = lowpass.astype(F32)
    by_device = dual.reshape(subbands, groups, share, capacity, columns)

    def run(choice, cap):
        def body():
            pieces = cut(facet_rows, image_cube, groups // 2, cap)
            made, windows, above, below = whole(
                facet_rows, lows, thresholds, pieces, image_cube, by_device, cap, choice
            )
            prior_term, updated = join(facet_rows, windows, above, below, made, band_rows)
            return updated.reshape(dual.shape), prior_term

        return body

    most = jnp.max(facet_rows[:, ::2] + facet_rows[:, 1::2]) + 2 * HALO
    mean = 2 * band_rows // groups
    steps = [mean, (mean + 2 * capacity) // 2, 2 * capacity]
    caps = [-(-(rows + 2 * HALO) // 8) * 8 for rows in steps]
    choice = (most > caps[0]).astype(jnp.int32) + (most > caps[1]).astype(jnp.int32)
    return lax.switch(choice, [run(i, cap) for i, cap in enumerate(caps)])


def solution(mesh):
    placed = (P("fac", "grp", None), P(None, None, ("grp", "fac"), None), P(), P(), P())
    return jax.shard_map(
        on_device,
        mesh=mesh,
        in_specs=placed,
        out_specs=(P(None, None, ("grp", "fac"), None), P("fac", "grp", None)),
        check_vma=False,
    )
```

```python
import functools

import jax
import jax.numpy as jnp
from jax import lax
from jax.experimental import pallas as pl
from jax.experimental.pallas import tpu as pltpu
from jax.sharding import PartitionSpec as P

HALO = 2
LEAD = 8
F32 = jnp.float32
BF16 = jnp.bfloat16
MESH = pl.DeviceIdType.MESH


def facet_starts(rows_ref):
    band = lax.axis_index("grp")
    starts = [jnp.int32(0)]
    for facet in range(rows_ref.shape[1]):
        starts.append(starts[-1] + rows_ref[band, facet])
    return starts


def position(chips):
    assert chips & (chips - 1) == 0
    facet = lax.axis_index("fac")
    core = lax.rem(facet, 2)
    chip = lax.div(facet, 2)
    sibling = facet + 1 - 2 * core

    def at(r):
        other = chip
        for bit in range(chips.bit_length() - 1):
            if r & 2**bit:
                other = other + 2**bit * (1 - 2 * lax.rem(lax.div(chip, 2**bit), 2))
        return other

    return core, chip, sibling, at


def remote(source, target, send, recv, device):
    return pltpu.make_async_remote_copy(
        src_ref=source, dst_ref=target, send_sem=send, recv_sem=recv,
        device_id=device, device_id_type=MESH,
    )


GROUP = 8


def tap(low_ref, d, a, k):
    count = low_ref.shape[1]
    high = low_ref[d, count - 1 - k] * (1.0 if k % 2 == 0 else -1.0)
    return jnp.where(a == 0, low_ref[d, k], high)


def moved(x, amount, way):
    amounts = jnp.full(x.shape, amount, jnp.int32)
    for bit in range(7):
        if 2**bit >= x.shape[0]:
            break
        turned = pltpu.roll(x, 2**bit if way > 0 else x.shape[0] - 2**bit, 0)
        x = jnp.where((amounts & 2**bit) != 0, turned, x)
    return x


def whole_kernel(
    cap, rows_ref, low_ref, thresholds_ref, cut_ref, image_ref, dual_ref,
    next_ref, windows, above_out, below_out,
    sent, own, other, arrived, stored, wide, strips, sums, terms, ahead, back,
    edge_above, edge_below, edge_spill,
    dual_sem, next_sem, edge_send, edge_recv,
    send, recv, pass_send, pass_recv, home_send, home_recv, sum_send, sum_recv,
):
    chips, share = sent.shape[:2]
    subbands, devices, _, capacity, columns = dual_ref.shape
    kinds = subbands // 2
    rows = image_ref.shape[1]
    flat = GROUP * capacity
    span = capacity + 8
    core, chip, sibling, at = position(chips)
    facet, band = lax.axis_index("fac"), lax.axis_index("grp")
    bands = lax.axis_size("grp")
    band_next, band_last = lax.rem(band + 1, bands), lax.rem(band + bands - 1, bands)

    def same_core(r):
        return {"fac": 2 * at(r) + core}

    def dual_load(c):
        return pltpu.make_async_copy(dual_ref.at[:, :, c], stored.at[c], dual_sem.at[c])

    def next_store(c):
        return pltpu.make_async_copy(stored.at[c], next_ref.at[:, :, c], next_sem.at[c])

    def remote_to(source, target, sends, recvs, r, c, device):
        return remote(source, target, sends.at[r, c], recvs.at[r, c], device)

    def outgoing(r, c):
        return remote_to(sent.at[at(r), c], own.at[chip, c], send, recv, r, c, same_core(r))

    def incoming(r, c):
        source = at(r)
        return remote_to(sent.at[source, c], own.at[source, c], send, recv, r, c, same_core(r))

    def passing(r, c):
        source = at(r)
        return remote_to(
            own.at[source, c], other.at[source, c], pass_send, pass_recv, r, c, {"fac": sibling}
        )

    def homing(r, c):
        return remote_to(
            other.at[at(r), c], arrived.at[at(r), c], home_send, home_recv, r, c,
            {"fac": sibling},
        )

    def returning(r, c):
        return remote_to(
            own.at[at(r), c], windows.at[chip, c], sum_send, sum_recv, r, c, same_core(r)
        )

    def returned(r, c):
        source = at(r)
        return remote_to(
            own.at[source, c], windows.at[source, c], sum_send, sum_recv, r, c, same_core(r)
        )

    barrier = pltpu.get_barrier_semaphore()
    for device in [same_core(r) for r in range(1, chips)] + [
        {"fac": sibling}, {"grp": band_next}, {"grp": band_last},
    ]:
        pl.semaphore_signal(barrier, inc=1, device_id=device, device_id_type=MESH)
    pl.semaphore_wait(barrier, chips + 2)

    rims = [
        remote(image_ref.at[:, rows - 8 : rows], edge_above, edge_send.at[0], edge_recv.at[0],
               {"grp": band_next}),
        remote(image_ref.at[:, 0:8], edge_below, edge_send.at[1], edge_recv.at[1],
               {"grp": band_last}),
    ]
    for rim in rims:
        rim.start()

    into = lax.broadcasted_iota(jnp.int32, (columns, columns), 0)
    of = lax.broadcasted_iota(jnp.int32, (columns, columns), 1)

    def build(d, _):
        for b in range(2):
            forward = jnp.zeros((columns, columns), F32)
            adjoint = jnp.zeros((columns, columns), F32)
            for k in range(2 * HALO):
                value = tap(low_ref, d, b, k)
                forward = jnp.where(into - of + HALO == k, value, forward)
                adjoint = jnp.where(of - into + HALO == k, value, adjoint)
            forward = forward.astype(BF16)
            ahead[d, 0:columns, b * columns : (b + 1) * columns] = forward
            ahead[d, columns : 2 * columns, b * columns : (b + 1) * columns] = forward
            back[d, b * columns : (b + 1) * columns, :] = adjoint.astype(BF16)
        return 0

    starts = facet_starts(rows_ref)
    last_rows = starts[2 * chips] - starts[2 * chips - 2]
    for rim in rims:
        rim.wait()
    row = lax.broadcasted_iota(jnp.int32, (cap, columns), 0)

    def rimmed(pair, c):
        window = cut_ref[pair, c]
        fill = jnp.zeros((cap - HALO, columns), F32)
        above = jnp.concatenate([edge_above[c, 8 - HALO : 8, :], fill], 0)
        first = (row < HALO) & (pair == 0) & (band > 0)
        window = jnp.where(first, above, window)
        for i in range(HALO - 1):
            below = jnp.broadcast_to(edge_below[c, i : i + 1, :], (cap, columns))
            last = (row == HALO + last_rows + i) & (pair == chips - 1) & (band < bands - 1)
            window = jnp.where(last, below, window)
        return window

    def cut(c, _):
        for r in list(range(chips - 1, -1, -1)):
            if r:
                sent[at(r), c] = rimmed(at(r), c)
                outgoing(r, c).start()
            else:
                own[chip, c] = rimmed(chip, c)
                passing(0, c).start()
        return 0

    lax.fori_loop(0, share, cut, 0)
    for c in range(share):
        dual_load(c).start()
    lax.fori_loop(0, low_ref.shape[0], build, 0)
    sums[...] = jnp.zeros_like(sums)

    offset = jnp.where(core == 0, 0, rows_ref[band, facet - core])
    length = rows_ref[band, facet]
    keep = lax.broadcasted_iota(jnp.int32, (capacity, columns), 0) < length

    def analyse(c, _):
        for r in range(chips - 1, 0, -1):
            incoming(r, c).wait_recv()
            passing(r, c).start()
        for r in range(chips):
            passing(r, c).wait_recv()
        dual_load(c).wait()
        for g in range(devices // GROUP):
            for source, half in ((own, core), (other, 1 - core)):
                for j in range(GROUP // 2):
                    window = source[g * (GROUP // 2) + j, c]
                    strips[2 * j + half] = moved(window, offset, -1)[:span]

            def one_kind(step, _):
                d, a = step // 2, step % 2
                sent_rows = tap(low_ref, d, a, 0) * strips[:, 0:capacity, :]
                for k in range(1, 2 * HALO):
                    sent_rows += tap(low_ref, d, a, k) * strips[:, k : k + capacity, :]
                flat_rows = sent_rows.reshape(flat, columns)
                high = flat_rows.astype(BF16)
                low = (flat_rows - high.astype(F32)).astype(BF16)
                both = jnp.concatenate([high, low], axis=1)
                coefficient = jnp.dot(both, ahead[d], preferred_element_type=F32)
                for b in range(2):
                    part = coefficient[:, b * columns : (b + 1) * columns]
                    part = part.reshape(GROUP, capacity, columns)
                    here = pl.ds(g * GROUP, GROUP)
                    u = stored[c, 2 * step + b, here].astype(F32) + part
                    u = jnp.where(keep, u, 0.0)
                    wide[c, 2 * step + b, here] = u
                    sums[2 * step + b] += jnp.sum(u * u, axis=0)
                return 0

            lax.fori_loop(0, kinds, one_kind, 0)
        return 0

    lax.fori_loop(0, share, analyse, 0)

    def scale(s, _):
        radius = thresholds_ref[s]
        sums[s] = radius / jnp.maximum(jnp.sqrt(sums[s]), radius)
        return 0

    lax.fori_loop(0, subbands, scale, 0)

    def settle(c, _):
        for r in range(chips):
            passing(r, c).wait_send()
            if r:
                outgoing(r, c).wait_send()
        return 0

    lax.fori_loop(0, share, settle, 0)

    def synthesise(c, _):
        for g in range(devices // GROUP):
            here = pl.ds(g * GROUP, GROUP)

            def one_kind(step, _):
                parts = []
                for b in range(2):
                    scaled = (wide[c, 2 * step + b, here] * sums[2 * step + b]).astype(BF16)
                    stored[c, 2 * step + b, here] = scaled
                    parts.append(scaled.reshape(flat, columns))
                both = jnp.concatenate(parts, axis=1)
                term = jnp.dot(both, back[step // 2], preferred_element_type=F32)
                terms[step] = term.reshape(GROUP, capacity, columns)
                return 0

            lax.fori_loop(0, kinds, one_kind, 0)
            for target, half in ((own, core), (other, 1 - core)):
                def place(j, _, target=target, half=half):
                    loaded = [terms[step, 2 * j + half] for step in range(kinds)]
                    merged = jnp.zeros((span, columns), F32)
                    for k in range(2 * HALO):
                        tap_sum = tap(low_ref, 0, 0, k) * loaded[0]
                        for step in range(1, kinds):
                            tap_sum += tap(low_ref, step // 2, step % 2, k) * loaded[step]
                        spare = jnp.zeros((span - capacity, columns), F32)
                        tall = jnp.concatenate([tap_sum, spare], 0)
                        merged += pltpu.roll(tall, k, 0) if k else tall
                    merged = jnp.concatenate([merged, jnp.zeros((cap - span, columns), F32)], 0)
                    target[g * (GROUP // 2) + j, c] = moved(merged, offset, 1)
                    return 0

                lax.fori_loop(0, GROUP // 2, place, 0)
        for r in list(range(chips - 1, -1, -1)):
            homing(r, c).start()
        next_store(c).start()
        for r in list(range(chips - 1, -1, -1)):
            homing(r, c).wait_recv()
            if r:
                own[at(r), c] = own[at(r), c] + arrived[at(r), c]
                returning(r, c).start()
            else:
                windows[chip, c] = own[chip, c] + arrived[chip, c]
        return 0

    lax.fori_loop(0, share, synthesise, 0)

    def finish(c, _):
        for r in range(chips):
            homing(r, c).wait_send()
            if r:
                returned(r, c).wait_recv()
                returning(r, c).wait_send()
        next_store(c).wait()
        return 0

    lax.fori_loop(0, share, finish, 0)

    for c in range(share):
        edge_spill[c] = jnp.zeros((8, columns), F32)
        for i in range(HALO - 1):
            found = jnp.where(row == HALO + last_rows + i, windows[chips - 1, c], 0.0)
            edge_spill[c, i : i + 1, :] = jnp.sum(found, axis=0, keepdims=True)
    spills = [
        remote(edge_spill, above_out, edge_send.at[2], edge_recv.at[2], {"grp": band_next}),
        remote(windows.at[0, :, 0:8], below_out, edge_send.at[3], edge_recv.at[3],
               {"grp": band_last}),
    ]
    for spill in spills:
        spill.start()
    for spill in spills:
        spill.wait()


def whole(facet_rows, lows, thresholds, pieces, image, dual, cap, collective_id):
    subbands, devices, share, capacity, columns = dual.shape
    chips, kinds = devices // 2, subbands // 2
    smem = pl.BlockSpec(memory_space=pltpu.SMEM)
    vmem = pl.BlockSpec(memory_space=pltpu.VMEM)
    free = pl.BlockSpec(memory_space=pl.ANY)
    windows = (chips, share, cap, columns)
    rim = jax.ShapeDtypeStruct((share, 8, columns), F32)
    dma = pltpu.SemaphoreType.DMA
    return pl.pallas_call(
        functools.partial(whole_kernel, cap),
        out_shape=(
            jax.ShapeDtypeStruct(dual.shape, dual.dtype), jax.ShapeDtypeStruct(windows, F32),
            rim, rim,
        ),
        in_specs=[smem, smem, smem, vmem, free, free],
        out_specs=(free, vmem, vmem, vmem),
        scratch_shapes=[
            *[pltpu.VMEM(windows, F32)] * 4,
            pltpu.VMEM((share, subbands, devices, capacity, columns), BF16),
            pltpu.VMEM((share, subbands, devices, capacity, columns), F32),
            pltpu.VMEM((GROUP, capacity + 8, columns), F32),
            pltpu.VMEM((subbands, capacity, columns), F32),
            pltpu.VMEM((kinds, GROUP, capacity, columns), F32),
            pltpu.VMEM((kinds // 2, 2 * columns, 2 * columns), BF16),
            pltpu.VMEM((kinds // 2, 2 * columns, columns), BF16),
            *[pltpu.VMEM((share, 8, columns), F32)] * 3,
            dma((share,)), dma((share,)), dma((4,)), dma((4,)),
            *[dma((chips, share))] * 8,
        ],
        compiler_params=pltpu.CompilerParams(
            collective_id=collective_id, has_side_effects=True, vmem_limit_bytes=62 * 2**20
        ),
    )(facet_rows, lows, thresholds, pieces, image, dual)


def cut_kernel(cap, rows_ref, image_ref, out_ref, padded):
    rows = image_ref.shape[1]
    share, _, columns = padded.shape
    padded[:, 0:LEAD, :] = jnp.zeros((share, LEAD, columns), F32)
    tail = padded.shape[1] - LEAD - rows
    padded[:, LEAD + rows :, :] = jnp.zeros((share, tail, columns), F32)
    padded[:, LEAD : LEAD + rows, :] = image_ref[...]
    starts = facet_starts(rows_ref)

    for pair in range(out_ref.shape[0]):
        begin = starts[2 * pair] + (LEAD - HALO)
        base = pl.multiple_of((begin // 8) * 8, 8)
        turn = cap + 8 - (begin - base)

        @pl.loop(0, out_ref.shape[1])
        def _(channel):
            window = padded[channel, pl.ds(base, cap + 8), :]
            out_ref[pair, channel] = pltpu.roll(window, turn, 0)[:cap]


def cut(facet_rows, image, pairs, cap):
    channels, rows, columns = image.shape
    vmem = pl.BlockSpec(memory_space=pltpu.VMEM)
    return pl.pallas_call(
        functools.partial(cut_kernel, cap),
        out_shape=jax.ShapeDtypeStruct((pairs, channels, cap, columns), F32),
        in_specs=[pl.BlockSpec(memory_space=pltpu.SMEM), vmem],
        out_specs=vmem,
        scratch_shapes=[pltpu.VMEM((channels, LEAD + rows + cap + 16, columns), F32)],
        compiler_params=pltpu.CompilerParams(vmem_limit_bytes=48 * 2**20),
    )(facet_rows, image)


def join_kernel(
    cap, rows_ref, windows_ref, above_ref, below_ref, made_ref, out_ref, next_ref,
    padded, staged, load_sems, store_sems,
):
    rows = out_ref.shape[1]
    subbands = made_ref.shape[0]
    loads = [
        pltpu.make_async_copy(made_ref.at[s], staged.at[s], load_sems.at[s])
        for s in range(subbands)
    ]
    stores = [
        pltpu.make_async_copy(staged.at[s], next_ref.at[s], store_sems.at[s])
        for s in range(subbands)
    ]
    for load in loads:
        load.start()
    padded[...] = jnp.zeros_like(padded)
    starts = facet_starts(rows_ref)
    band, bands = lax.axis_index("grp"), lax.axis_size("grp")

    for pair in range(windows_ref.shape[0]):
        begin = starts[2 * pair] + (LEAD - HALO)
        base = pl.multiple_of((begin // 8) * 8, 8)

        @pl.loop(0, windows_ref.shape[1])
        def _(channel):
            window = windows_ref[pair, channel]
            window = jnp.concatenate([window, jnp.zeros((8, window.shape[1]), F32)], 0)
            here = (channel, pl.ds(base, cap + 8), slice(None))
            padded[here] = padded[here] + pltpu.roll(window, begin - base, 0)

        pairs = windows_ref.shape[0]
        for s in range(pair * subbands // pairs, (pair + 1) * subbands // pairs):
            loads[s].wait()
            stores[s].start()

    out_ref[...] = padded[:, LEAD : LEAD + rows, :]
    above = jnp.where(band > 0, above_ref[:, 0:HALO, :], 0.0)
    below = jnp.where(band < bands - 1, below_ref[:, 0:HALO, :], 0.0)
    out_ref[:, 0:HALO, :] = out_ref[:, 0:HALO, :] + above
    out_ref[:, rows - HALO : rows, :] = out_ref[:, rows - HALO : rows, :] + below
    for store in stores:
        store.wait()


def join(facet_rows, windows, above, below, made, rows):
    pairs, channels, cap, columns = windows.shape
    vmem = pl.BlockSpec(memory_space=pltpu.VMEM)
    free = pl.BlockSpec(memory_space=pl.ANY)
    return pl.pallas_call(
        functools.partial(join_kernel, cap),
        out_shape=(
            jax.ShapeDtypeStruct((channels, rows, columns), F32),
            jax.ShapeDtypeStruct(made.shape, made.dtype),
        ),
        in_specs=[pl.BlockSpec(memory_space=pltpu.SMEM), vmem, vmem, vmem, free],
        out_specs=(vmem, free),
        scratch_shapes=[
            pltpu.VMEM((channels, LEAD + rows + cap + 16, columns), F32),
            pltpu.VMEM(made.shape, made.dtype),
            pltpu.SemaphoreType.DMA((made.shape[0],)),
            pltpu.SemaphoreType.DMA((made.shape[0],)),
        ],
        compiler_params=pltpu.CompilerParams(vmem_limit_bytes=48 * 2**20),
    )(facet_rows, windows, above, below, made)


def on_device(image_cube, dual, lowpass, thresholds, facet_rows):
    groups = lax.axis_size("fac")
    share, band_rows, _ = image_cube.shape
    subbands, _, capacity, columns = dual.shape
    lows = lowpass.astype(F32)
    by_device = dual.reshape(subbands, groups, share, capacity, columns)

    def run(choice, cap):
        def body():
            pieces = cut(facet_rows, image_cube, groups // 2, cap)
            made, windows, above, below = whole(
                facet_rows, lows, thresholds, pieces, image_cube, by_device, cap, choice
            )
            prior_term, updated = join(facet_rows, windows, above, below, made, band_rows)
            return updated.reshape(dual.shape), prior_term

        return body

    most = jnp.max(jnp.sum(facet_rows.reshape(-1, 2), axis=1)) + 2 * HALO
    mean = 2 * band_rows // groups
    steps = [mean, (mean + 2 * capacity) // 2, 2 * capacity]
    caps = [-(-(rows + 2 * HALO) // 8) * 8 for rows in steps]
    choice = (most > caps[0]).astype(jnp.int32) + (most > caps[1]).astype(jnp.int32)
    return lax.switch(choice, [run(i, cap) for i, cap in enumerate(caps)])


def solution(mesh):
    placed = (P("fac", "grp", None), P(None, None, ("grp", "fac"), None), P(), P(), P())
    return jax.shard_map(
        on_device,
        mesh=mesh,
        in_specs=placed,
        out_specs=(P(None, None, ("grp", "fac"), None), P("fac", "grp", None)),
        check_vma=False,
    )
```

```python
import functools

import jax
import jax.numpy as jnp
from jax import lax
from jax.experimental import pallas as pl
from jax.experimental.pallas import tpu as pltpu
from jax.sharding import PartitionSpec as P

HALO = 2
LEAD = 8
F32 = jnp.float32
BF16 = jnp.bfloat16
MESH = pl.DeviceIdType.MESH


def facet_starts(rows_ref):
    band = lax.axis_index("grp")
    starts = [jnp.int32(0)]
    for facet in range(rows_ref.shape[1]):
        starts.append(starts[-1] + rows_ref[band, facet])
    return starts


def position(chips):
    assert chips & (chips - 1) == 0
    facet = lax.axis_index("fac")
    core = lax.rem(facet, 2)
    chip = lax.div(facet, 2)
    sibling = facet + 1 - 2 * core

    def at(r):
        other = chip
        for bit in range(chips.bit_length() - 1):
            if r & 2**bit:
                other = other + 2**bit * (1 - 2 * lax.rem(lax.div(chip, 2**bit), 2))
        return other

    return core, chip, sibling, at


def remote(source, target, send, recv, device):
    return pltpu.make_async_remote_copy(
        src_ref=source, dst_ref=target, send_sem=send, recv_sem=recv,
        device_id=device, device_id_type=MESH,
    )


GROUP = 8


def tap(low_ref, d, a, k):
    count = low_ref.shape[1]
    high = low_ref[d, count - 1 - k] * (1.0 if k % 2 == 0 else -1.0)
    return jnp.where(a == 0, low_ref[d, k], high)


def moved(x, amount, way):
    amounts = jnp.full(x.shape, amount, jnp.int32)
    for bit in range(7):
        if 2**bit >= x.shape[0]:
            break
        turned = pltpu.roll(x, 2**bit if way > 0 else x.shape[0] - 2**bit, 0)
        x = jnp.where((amounts & 2**bit) != 0, turned, x)
    return x


def whole_kernel(
    cap, rows_ref, low_ref, thresholds_ref, cut_ref, image_ref, dual_ref,
    next_ref, windows, above_out, below_out,
    sent, own, other, arrived, stored, wide, strips, sums, terms, ahead, back,
    edge_above, edge_below, edge_spill,
    cut_sem, dual_sem, next_sem, edge_send, edge_recv,
    send, recv, pass_send, pass_recv, home_send, home_recv, sum_send, sum_recv,
):
    chips, share = sent.shape[:2]
    subbands, devices, _, capacity, columns = dual_ref.shape
    kinds = subbands // 2
    rows = image_ref.shape[1]
    flat = GROUP * capacity
    span = capacity + 8
    core, chip, sibling, at = position(chips)
    facet, band = lax.axis_index("fac"), lax.axis_index("grp")
    bands = lax.axis_size("grp")
    band_next, band_last = lax.rem(band + 1, bands), lax.rem(band + bands - 1, bands)

    def same_core(r):
        return {"fac": 2 * at(r) + core}

    def dual_load(c):
        return pltpu.make_async_copy(dual_ref.at[:, :, c], stored.at[c], dual_sem.at[c])

    def next_store(c):
        return pltpu.make_async_copy(stored.at[c], next_ref.at[:, :, c], next_sem.at[c])

    def remote_to(source, target, sends, recvs, r, c, device):
        return remote(source, target, sends.at[r, c], recvs.at[r, c], device)

    def outgoing(r, c):
        return remote_to(sent.at[at(r), c], own.at[chip, c], send, recv, r, c, same_core(r))

    def incoming(r, c):
        source = at(r)
        return remote_to(sent.at[source, c], own.at[source, c], send, recv, r, c, same_core(r))

    def passing(r, c):
        source = at(r)
        return remote_to(
            own.at[source, c], other.at[source, c], pass_send, pass_recv, r, c, {"fac": sibling}
        )

    def homing(r, c):
        return remote_to(
            other.at[at(r), c], arrived.at[at(r), c], home_send, home_recv, r, c,
            {"fac": sibling},
        )

    def returning(r, c):
        return remote_to(
            own.at[at(r), c], windows.at[chip, c], sum_send, sum_recv, r, c, same_core(r)
        )

    def returned(r, c):
        source = at(r)
        return remote_to(
            own.at[source, c], windows.at[source, c], sum_send, sum_recv, r, c, same_core(r)
        )

    cut_load = pltpu.make_async_copy(cut_ref, sent, cut_sem)
    cut_load.start()
    barrier = pltpu.get_barrier_semaphore()
    for device in [same_core(r) for r in range(1, chips)] + [
        {"fac": sibling}, {"grp": band_next}, {"grp": band_last},
    ]:
        pl.semaphore_signal(barrier, inc=1, device_id=device, device_id_type=MESH)
    pl.semaphore_wait(barrier, chips + 2)

    rims = [
        remote(image_ref.at[:, rows - 8 : rows], edge_above, edge_send.at[0], edge_recv.at[0],
               {"grp": band_next}),
        remote(image_ref.at[:, 0:8], edge_below, edge_send.at[1], edge_recv.at[1],
               {"grp": band_last}),
    ]
    for rim in rims:
        rim.start()

    into = lax.broadcasted_iota(jnp.int32, (columns, columns), 0)
    of = lax.broadcasted_iota(jnp.int32, (columns, columns), 1)

    def build(d, _):
        for b in range(2):
            forward = jnp.zeros((columns, columns), F32)
            adjoint = jnp.zeros((columns, columns), F32)
            for k in range(2 * HALO):
                value = tap(low_ref, d, b, k)
                forward = jnp.where(into - of + HALO == k, value, forward)
                adjoint = jnp.where(of - into + HALO == k, value, adjoint)
            forward = forward.astype(BF16)
            ahead[d, 0:columns, b * columns : (b + 1) * columns] = forward
            ahead[d, columns : 2 * columns, b * columns : (b + 1) * columns] = forward
            back[d, b * columns : (b + 1) * columns, :] = adjoint.astype(BF16)
        return 0

    starts = facet_starts(rows_ref)
    last_rows = starts[2 * chips] - starts[2 * chips - 2]
    cut_load.wait()
    inner = [(at(r) > 0) & (at(r) < chips - 1) for r in range(chips)]
    for r in range(chips - 1, 0, -1):
        @pl.when(inner[r])
        def _(r=r):
            outgoing(r, 0).start()
    for rim in rims:
        rim.wait()
    row = lax.broadcasted_iota(jnp.int32, (cap, columns), 0)

    def rimmed(pair, c):
        window = sent[pair, c]
        fill = jnp.zeros((cap - HALO, columns), F32)
        above = jnp.concatenate([edge_above[c, 8 - HALO : 8, :], fill], 0)
        first = (row < HALO) & (pair == 0) & (band > 0)
        window = jnp.where(first, above, window)
        for i in range(HALO - 1):
            below = jnp.broadcast_to(edge_below[c, i : i + 1, :], (cap, columns))
            last = (row == HALO + last_rows + i) & (pair == chips - 1) & (band < bands - 1)
            window = jnp.where(last, below, window)
        return window

    def cut(c, first):
        for r in range(chips - 1, -1, -1):
            @pl.when(jnp.logical_not(inner[r]))
            def _(r=r):
                sent[at(r), c] = rimmed(at(r), c)
                if r:
                    outgoing(r, c).start()

            if r and not first:
                @pl.when(inner[r])
                def _(r=r):
                    outgoing(r, c).start()

            if r == 0:
                own[chip, c] = sent[chip, c]
                passing(0, c).start()

    cut(0, True)
    if share > 1:
        @pl.loop(1, share)
        def _(c):
            cut(c, False)

    for c in range(share):
        dual_load(c).start()
    lax.fori_loop(0, low_ref.shape[0], build, 0)
    sums[...] = jnp.zeros_like(sums)

    offset = jnp.where(core == 0, 0, rows_ref[band, facet - core])
    length = rows_ref[band, facet]
    keep = lax.broadcasted_iota(jnp.int32, (capacity, columns), 0) < length

    def analyse(c, _):
        for r in range(chips - 1, 0, -1):
            incoming(r, c).wait_recv()
            passing(r, c).start()
        for r in range(chips):
            passing(r, c).wait_recv()
        dual_load(c).wait()
        for g in range(devices // GROUP):
            for source, half in ((own, core), (other, 1 - core)):
                for j in range(GROUP // 2):
                    window = source[g * (GROUP // 2) + j, c]
                    strips[2 * j + half] = moved(window, offset, -1)[:span]

            def one_kind(step, _):
                d, a = step // 2, step % 2
                sent_rows = tap(low_ref, d, a, 0) * strips[:, 0:capacity, :]
                for k in range(1, 2 * HALO):
                    sent_rows += tap(low_ref, d, a, k) * strips[:, k : k + capacity, :]
                flat_rows = sent_rows.reshape(flat, columns)
                high = flat_rows.astype(BF16)
                low = (flat_rows - high.astype(F32)).astype(BF16)
                both = jnp.concatenate([high, low], axis=1)
                coefficient = jnp.dot(both, ahead[d], preferred_element_type=F32)
                for b in range(2):
                    part = coefficient[:, b * columns : (b + 1) * columns]
                    part = part.reshape(GROUP, capacity, columns)
                    here = pl.ds(g * GROUP, GROUP)
                    u = stored[c, 2 * step + b, here].astype(F32) + part
                    u = jnp.where(keep, u, 0.0)
                    wide[c, 2 * step + b, here] = u
                    sums[2 * step + b] += jnp.sum(u * u, axis=0)
                return 0

            lax.fori_loop(0, kinds, one_kind, 0)
        return 0

    lax.fori_loop(0, share, analyse, 0)

    def scale(s, _):
        radius = thresholds_ref[s]
        sums[s] = radius / jnp.maximum(jnp.sqrt(sums[s]), radius)
        return 0

    lax.fori_loop(0, subbands, scale, 0)

    def settle(c, _):
        for r in range(chips):
            passing(r, c).wait_send()
            if r:
                outgoing(r, c).wait_send()
        return 0

    lax.fori_loop(0, share, settle, 0)

    def synthesise(c, _):
        for g in range(devices // GROUP):
            here = pl.ds(g * GROUP, GROUP)

            def one_kind(step, _):
                parts = []
                for b in range(2):
                    scaled = (wide[c, 2 * step + b, here] * sums[2 * step + b]).astype(BF16)
                    stored[c, 2 * step + b, here] = scaled
                    parts.append(scaled.reshape(flat, columns))
                both = jnp.concatenate(parts, axis=1)
                term = jnp.dot(both, back[step // 2], preferred_element_type=F32)
                terms[step] = term.reshape(GROUP, capacity, columns)
                return 0

            lax.fori_loop(0, kinds, one_kind, 0)
            for target, half in ((other, 1 - core), (own, core)):
                def place(j, _, target=target, half=half):
                    loaded = [terms[step, 2 * j + half] for step in range(kinds)]
                    merged = jnp.zeros((span, columns), F32)
                    for k in range(2 * HALO):
                        tap_sum = tap(low_ref, 0, 0, k) * loaded[0]
                        for step in range(1, kinds):
                            tap_sum += tap(low_ref, step // 2, step % 2, k) * loaded[step]
                        spare = jnp.zeros((span - capacity, columns), F32)
                        tall = jnp.concatenate([tap_sum, spare], 0)
                        merged += pltpu.roll(tall, k, 0) if k else tall
                    merged = jnp.concatenate([merged, jnp.zeros((cap - span, columns), F32)], 0)
                    target[g * (GROUP // 2) + j, c] = moved(merged, offset, 1)
                    return 0

                lax.fori_loop(0, GROUP // 2, place, 0)
                if target is other and g == devices // GROUP - 1:
                    for r in range(chips - 1, -1, -1):
                        homing(r, c).start()
        next_store(c).start()
        for r in list(range(chips - 1, -1, -1)):
            homing(r, c).wait_recv()
            if r:
                own[at(r), c] = own[at(r), c] + arrived[at(r), c]
                returning(r, c).start()
            else:
                windows[chip, c] = own[chip, c] + arrived[chip, c]
        return 0

    lax.fori_loop(0, share, synthesise, 0)

    def finish(c, _):
        for r in range(chips):
            homing(r, c).wait_send()
            if r:
                returned(r, c).wait_recv()
                returning(r, c).wait_send()
        next_store(c).wait()
        return 0

    lax.fori_loop(0, share, finish, 0)

    for c in range(share):
        edge_spill[c] = jnp.zeros((8, columns), F32)
        for i in range(HALO - 1):
            found = jnp.where(row == HALO + last_rows + i, windows[chips - 1, c], 0.0)
            edge_spill[c, i : i + 1, :] = jnp.sum(found, axis=0, keepdims=True)
    spills = [
        remote(edge_spill, above_out, edge_send.at[2], edge_recv.at[2], {"grp": band_next}),
        remote(windows.at[0, :, 0:8], below_out, edge_send.at[3], edge_recv.at[3],
               {"grp": band_last}),
    ]
    for spill in spills:
        spill.start()
    for spill in spills:
        spill.wait()


def whole(facet_rows, lows, thresholds, pieces, image, dual, cap, collective_id):
    subbands, devices, share, capacity, columns = dual.shape
    chips, kinds = devices // 2, subbands // 2
    smem = pl.BlockSpec(memory_space=pltpu.SMEM)
    vmem = pl.BlockSpec(memory_space=pltpu.VMEM)
    free = pl.BlockSpec(memory_space=pl.ANY)
    windows = (chips, share, cap, columns)
    rim = jax.ShapeDtypeStruct((share, 8, columns), F32)
    dma = pltpu.SemaphoreType.DMA
    return pl.pallas_call(
        functools.partial(whole_kernel, cap),
        out_shape=(
            jax.ShapeDtypeStruct(dual.shape, dual.dtype), jax.ShapeDtypeStruct(windows, F32),
            rim, rim,
        ),
        in_specs=[smem, smem, smem, free, free, free],
        out_specs=(free, vmem, vmem, vmem),
        scratch_shapes=[
            *[pltpu.VMEM(windows, F32)] * 4,
            pltpu.VMEM((share, subbands, devices, capacity, columns), BF16),
            pltpu.VMEM((share, subbands, devices, capacity, columns), F32),
            pltpu.VMEM((GROUP, capacity + 8, columns), F32),
            pltpu.VMEM((subbands, capacity, columns), F32),
            pltpu.VMEM((kinds, GROUP, capacity, columns), F32),
            pltpu.VMEM((kinds // 2, 2 * columns, 2 * columns), BF16),
            pltpu.VMEM((kinds // 2, 2 * columns, columns), BF16),
            *[pltpu.VMEM((share, 8, columns), F32)] * 3,
            dma, dma((share,)), dma((share,)), dma((4,)), dma((4,)),
            *[dma((chips, share))] * 8,
        ],
        compiler_params=pltpu.CompilerParams(
            collective_id=collective_id, has_side_effects=True, vmem_limit_bytes=62 * 2**20
        ),
    )(facet_rows, lows, thresholds, pieces, image, dual)


def cut_kernel(cap, rows_ref, image_ref, out_ref, padded):
    rows = image_ref.shape[1]
    share, _, columns = padded.shape
    padded[:, 0:LEAD, :] = jnp.zeros((share, LEAD, columns), F32)
    tail = padded.shape[1] - LEAD - rows
    padded[:, LEAD + rows :, :] = jnp.zeros((share, tail, columns), F32)
    padded[:, LEAD : LEAD + rows, :] = image_ref[...]
    starts = facet_starts(rows_ref)

    for pair in range(out_ref.shape[0]):
        begin = starts[2 * pair] + (LEAD - HALO)
        base = pl.multiple_of((begin // 8) * 8, 8)
        turn = cap + 8 - (begin - base)

        @pl.loop(0, out_ref.shape[1])
        def _(channel):
            window = padded[channel, pl.ds(base, cap + 8), :]
            out_ref[pair, channel] = pltpu.roll(window, turn, 0)[:cap]


def cut(facet_rows, image, pairs, cap):
    channels, rows, columns = image.shape
    vmem = pl.BlockSpec(memory_space=pltpu.VMEM)
    return pl.pallas_call(
        functools.partial(cut_kernel, cap),
        out_shape=jax.ShapeDtypeStruct((pairs, channels, cap, columns), F32),
        in_specs=[pl.BlockSpec(memory_space=pltpu.SMEM), vmem],
        out_specs=vmem,
        scratch_shapes=[pltpu.VMEM((channels, LEAD + rows + cap + 16, columns), F32)],
        compiler_params=pltpu.CompilerParams(vmem_limit_bytes=48 * 2**20),
    )(facet_rows, image)


def join_kernel(
    cap, rows_ref, windows_hbm, above_hbm, below_hbm, made_ref, out_ref, next_ref,
    padded, staged, windows_ref, above_ref, below_ref, load_sems, store_sems, part_sems,
):
    rows = out_ref.shape[1]
    subbands = made_ref.shape[0]
    loads = [
        pltpu.make_async_copy(made_ref.at[s], staged.at[s], load_sems.at[s])
        for s in range(subbands)
    ]
    stores = [
        pltpu.make_async_copy(staged.at[s], next_ref.at[s], store_sems.at[s])
        for s in range(subbands)
    ]
    parts = [
        pltpu.make_async_copy(source, target, part_sems.at[i])
        for i, (source, target) in enumerate(
            [(windows_hbm, windows_ref), (above_hbm, above_ref), (below_hbm, below_ref)]
        )
    ]
    for copy in parts + loads:
        copy.start()
    padded[...] = jnp.zeros_like(padded)
    starts = facet_starts(rows_ref)
    band, bands = lax.axis_index("grp"), lax.axis_size("grp")

    for copy in parts:
        copy.wait()
    for pair in range(windows_ref.shape[0]):
        begin = starts[2 * pair] + (LEAD - HALO)
        base = pl.multiple_of((begin // 8) * 8, 8)

        @pl.loop(0, windows_ref.shape[1])
        def _(channel):
            window = windows_ref[pair, channel]
            window = jnp.concatenate([window, jnp.zeros((8, window.shape[1]), F32)], 0)
            here = (channel, pl.ds(base, cap + 8), slice(None))
            padded[here] = padded[here] + pltpu.roll(window, begin - base, 0)

        pairs = windows_ref.shape[0]
        for s in range(pair * subbands // pairs, (pair + 1) * subbands // pairs):
            loads[s].wait()
            stores[s].start()

    out_ref[...] = padded[:, LEAD : LEAD + rows, :]
    above = jnp.where(band > 0, above_ref[:, 0:HALO, :], 0.0)
    below = jnp.where(band < bands - 1, below_ref[:, 0:HALO, :], 0.0)
    out_ref[:, 0:HALO, :] = out_ref[:, 0:HALO, :] + above
    out_ref[:, rows - HALO : rows, :] = out_ref[:, rows - HALO : rows, :] + below
    for store in stores:
        store.wait()


def join(facet_rows, windows, above, below, made, rows):
    pairs, channels, cap, columns = windows.shape
    vmem = pl.BlockSpec(memory_space=pltpu.VMEM)
    free = pl.BlockSpec(memory_space=pl.ANY)
    return pl.pallas_call(
        functools.partial(join_kernel, cap),
        out_shape=(
            jax.ShapeDtypeStruct((channels, rows, columns), F32),
            jax.ShapeDtypeStruct(made.shape, made.dtype),
        ),
        in_specs=[pl.BlockSpec(memory_space=pltpu.SMEM), free, free, free, free],
        out_specs=(vmem, free),
        scratch_shapes=[
            pltpu.VMEM((channels, LEAD + rows + cap + 16, columns), F32),
            pltpu.VMEM(made.shape, made.dtype),
            pltpu.VMEM(windows.shape, F32),
            pltpu.VMEM(above.shape, F32),
            pltpu.VMEM(below.shape, F32),
            pltpu.SemaphoreType.DMA((made.shape[0],)),
            pltpu.SemaphoreType.DMA((made.shape[0],)),
            pltpu.SemaphoreType.DMA((3,)),
        ],
        compiler_params=pltpu.CompilerParams(vmem_limit_bytes=60 * 2**20),
    )(facet_rows, windows, above, below, made)


def on_device(image_cube, dual, lowpass, thresholds, facet_rows):
    groups = lax.axis_size("fac")
    share, band_rows, _ = image_cube.shape
    subbands, _, capacity, columns = dual.shape
    lows = lowpass.astype(F32)
    by_device = dual.reshape(subbands, groups, share, capacity, columns)

    def run(choice, cap):
        def body():
            pieces = cut(facet_rows, image_cube, groups // 2, cap)
            made, windows, above, below = whole(
                facet_rows, lows, thresholds, pieces, image_cube, by_device, cap, choice
            )
            prior_term, updated = join(facet_rows, windows, above, below, made, band_rows)
            return updated.reshape(dual.shape), prior_term

        return body

    most = jnp.max(jnp.sum(facet_rows.reshape(-1, 2), axis=1)) + 2 * HALO
    mean = 2 * band_rows // groups
    steps = [mean, (mean + 2 * capacity) // 2, 2 * capacity]
    caps = [-(-(rows + 2 * HALO) // 8) * 8 for rows in steps]
    choice = (most > caps[0]).astype(jnp.int32) + (most > caps[1]).astype(jnp.int32)
    return lax.switch(choice, [run(i, cap) for i, cap in enumerate(caps)])


def solution(mesh):
    placed = (P("fac", "grp", None), P(None, None, ("grp", "fac"), None), P(), P(), P())
    return jax.shard_map(
        on_device,
        mesh=mesh,
        in_specs=placed,
        out_specs=(P(None, None, ("grp", "fac"), None), P("fac", "grp", None)),
        check_vma=False,
    )
```
